32 devices in a mesh: groups: 2 (over x), lat: 16 (over z, y, core).
Axes of the slice: x: 2, y: 2, z: 4, core: 2. Of those that a mesh axis runs over, the one named last changes fastest.
Arguments:
- spectral: bfloat16 [384, 2, 2, 16, 384], P('lat', None, None, 'groups'), parts along dimension 3, may hold values from -6 to 6
- legendre: bfloat16 [384, 384, 768], P('lat'), may hold values from -0.3125 to 0.3125
- tracers: bfloat16 [768, 30, 16, 1536], P('lat', None, 'groups'), parts along dimension 2, may hold values from 0.19921875 to 2
- rates: float32 [30, 30], replicated, may hold values from -1 to 1
- decay: float32 [30, 8], replicated, may hold values from 0.05 to 2
Outputs:
- tracers_next: bfloat16 [768, 30, 16, 1536], P('lat', None, 'groups'), parts along dimension 2
The draws below stay inside these ranges and needn't reach their ends.
There are 2 independent parts, one for each index of `groups`. The reference program is written for one: setup_inputs(seed, part) draws one part's arguments, and reference() takes and returns one part's arrays. A program takes and returns all parts, laid end to end along the dimension named above; an argument that names none is the same for every part. Nothing has to cross between parts.
All inputs are finite; a program needn't handle non-finite values.
Results may differ from the reference program's by a relative error of at most 0.0029.
Values may be sent and summed in bfloat16 or wider, within the bound.
No kernel may reach another device: no remote copies, remote signals or barrier semaphores. Data moves between devices by JAX's collectives and lax.ppermute only.
A program may use at most 576 MiB of HBM per device.

```python
import math
import jax
import jax.numpy as jnp
from jax import lax

M = 384
NDEG = 384
NLAT = 768
NLON = 1536
NT = 30
K = 8


def level_of(stream_key, dims, shards, least, largest):
    gain, own = 1.0, jax.random.fold_in(stream_key, 6)
    for position, parts in shards:
        steps = jnp.exp(jax.random.uniform(jax.random.fold_in(own, position), (parts,), jnp.float32, least / len(shards), largest / len(shards)))
        gain = gain * jnp.repeat(steps, dims[position] // parts).reshape([-1 if axis == position else 1 for axis in range(len(dims))])
    return gain


def centred(rng, dims, scale, reach, pieces=(), held_as=jnp.bfloat16):
    drawn = jax.random.normal(rng, dims, jnp.float32) * scale
    if len(pieces) > 0:
        drawn = level_of(rng, dims, pieces, -0.22, 0.18) * drawn
    return jnp.clip(drawn, min=-reach, max=reach).astype(held_as)


def setup_inputs(seed: int = 0, part: int = 0) -> dict:
    keys = jax.random.split(jax.random.key(seed), 6)
    part_keys = jax.random.split(jax.random.fold_in(keys[5], part), 6)
    spectral = centred(part_keys[0], (M, 2, 2, K, NDEG), 1.0, 6.0, ((0, 16),))
    legendre = centred(keys[1], (M, NDEG, NLAT), NDEG ** -0.5, 0.3125, ((0, 16),))
    tracers = jnp.clip(0.19921875 + 1.8007812 * jax.random.uniform(part_keys[2], (NLAT, NT, K, NLON), jnp.float32) ** level_of(part_keys[2], (NLAT, NT, K, NLON), ((0, 16),), -0.2, 0.2), 0.19921875, 2.0).astype(jnp.bfloat16)
    rates = centred(keys[3], (NT, NT), NT ** -0.5, 1.0, (), jnp.float32)
    decay = jnp.clip(jnp.exp(jax.random.uniform(keys[4], (NT, K), jnp.float32, math.log(0.05), math.log(2.0))), 0.05, 2.0)
    return dict(spectral=spectral, legendre=legendre, tracers=tracers, rates=rates, decay=decay)


COURANT = 0.45

def fourier_basis(wave_total, lon_count):
    wave_ids = lax.broadcasted_iota(jnp.int32, (wave_total, lon_count), 0)
    lon_ids = lax.broadcasted_iota(jnp.int32, (wave_total, lon_count), 1)
    phase = wave_ids * lon_ids % lon_count
    angle = phase.astype(jnp.float32) * (2.0 * math.pi / lon_count)
    factor = 1.0 / math.sqrt(wave_total)
    return jnp.stack([jnp.cos(angle) * factor, -jnp.sin(angle) * factor]).astype(jnp.bfloat16)

def limiter(speed):
    return COURANT * speed / (1.0 + jnp.abs(speed))

def advect(q_rows, east_rows, north_rows, rates, decay):
    field = q_rows.astype(jnp.float32)
    east_cells = east_rows.astype(jnp.float32)
    north_cells = north_rows.astype(jnp.float32)
    face_x = limiter(0.5 * (east_cells + jnp.roll(east_cells, -1, axis=2)))[:, None]
    face_y = limiter(0.5 * (north_cells[:-1] + north_cells[1:]))[:, None]
    centre = field[1:-1]
    flux_x = jnp.maximum(face_x, 0.0) * centre + jnp.minimum(face_x, 0.0) * jnp.roll(centre, -1, axis=3)
    flux_y = jnp.maximum(face_y, 0.0) * field[:-1] + jnp.minimum(face_y, 0.0) * field[1:]
    advected = centre - (flux_x - jnp.roll(flux_x, 1, axis=3)) - (flux_y[1:] - flux_y[:-1])
    coupled = jnp.einsum('ts,lskx->ltkx', rates, advected, precision=lax.Precision.HIGHEST)
    return (jnp.exp(-decay)[None, :, :, None] * advected + coupled).astype(jnp.bfloat16)

def reference(spectral, legendre, tracers, rates, decay):
    wave_total, deg_count, lat_count = legendre.shape
    lon_count = tracers.shape[3]

    def one_wave(packed):
        coeffs, legend_rows, wave = packed
        deg_ids = jnp.arange(deg_count, dtype=jnp.int32)[:, None]
        masked = jnp.where(deg_ids >= wave, legend_rows, jnp.zeros((), jnp.bfloat16))
        return jnp.einsum('rckn,nl->rckl', coeffs.astype(jnp.float32), masked.astype(jnp.float32)).astype(jnp.bfloat16)
    fourier = lax.map(one_wave, (spectral, legendre, jnp.arange(wave_total, dtype=jnp.int32)))
    basis = fourier_basis(wave_total, lon_count)
    winds = jnp.einsum('mrckl,rmx->lckx', fourier.astype(jnp.float32), basis.astype(jnp.float32)).astype(jnp.bfloat16)
    east_all = winds[:, 0]
    zero_wind = jnp.zeros((1,) + east_all.shape[1:], jnp.bfloat16)
    north_pad = jnp.concatenate([zero_wind, winds[:, 1], zero_wind], axis=0)
    zero_rim = jnp.zeros((1,) + tracers.shape[1:], jnp.bfloat16)
    q_padded = jnp.concatenate([zero_rim, tracers, zero_rim], axis=0)

    def one_row(row_index):
        q_three = lax.dynamic_slice_in_dim(q_padded, row_index, 3, 0)
        north_three = lax.dynamic_slice_in_dim(north_pad, row_index, 3, 0)
        east_one = lax.dynamic_slice_in_dim(east_all, row_index, 1, 0)
        return advect(q_three, east_one, north_three, rates, decay)[0]
    return lax.map(one_row, jnp.arange(lat_count, dtype=jnp.int32))
```

```python
import functools
import math

import jax
import jax.numpy as jnp
from jax import lax
from jax.experimental import pallas as pl
from jax.experimental.pallas import tpu as pltpu
from jax.sharding import PartitionSpec as P

COURANT = 0.45
BF = jnp.bfloat16
F32 = jnp.float32
LANES = 128
VMEM_LIMIT = 56 * 2**20


def divisor(count, most):
    return max(d for d in range(1, most + 1) if count % d == 0)


def tiles(ref, first, count):
    return jnp.concatenate([ref[j, pl.ds(first, count), :] for j in range(ref.shape[0])], axis=1)


def params():
    return pltpu.CompilerParams(vmem_limit_bytes=VMEM_LIMIT)


def legendre_kernel(waves, first_ref, spec_ref, leg_ref, out_ref, four_ref):
    step = pl.program_id(0)
    per_step, _, _, levels, degs = spec_ref.shape
    lats = leg_ref.shape[2]
    lines = spec_ref.shape[1] * spec_ref.shape[2] * levels
    deg = lax.broadcasted_iota(jnp.int32, (lines, degs), 1)
    for i in range(per_step):
        wave = step * per_step + i
        coeffs = spec_ref[i].astype(F32).reshape(lines, degs)
        coeffs = jnp.where(deg >= first_ref[0] + wave, coeffs, 0.0).astype(BF)
        res = jnp.dot(coeffs, leg_ref[i], preferred_element_type=F32)
        for j in range(lats // LANES):
            four_ref[j, pl.ds(wave, lines, stride=waves), :] = res[:, j * LANES : (j + 1) * LANES]

    @pl.when(step == pl.num_programs(0) - 1)
    def _():
        dests = out_ref.shape[0]
        rows = lats // dests
        half = lines // 2
        for ck in range(half):
            both = jnp.concatenate(
                [
                    tiles(four_ref, first, waves)
                    for first in (ck * waves, (half + ck) * waves)
                ],
                axis=0,
            ).astype(BF)
            for d in range(dests):
                out_ref[d, :, ck * rows : (ck + 1) * rows] = both[:, d * rows : (d + 1) * rows]


def legendre_synthesis(first, spectral, legendre, dests):
    waves, parts, comps, levels, degs = spectral.shape
    lats = legendre.shape[2]
    per_step = divisor(waves, 4)
    rows = lats // dests
    lines = parts * comps * levels
    return pl.pallas_call(
        functools.partial(legendre_kernel, waves),
        grid=(waves // per_step,),
        in_specs=[
            pl.BlockSpec(memory_space=pltpu.SMEM),
            pl.BlockSpec((per_step, parts, comps, levels, degs), lambda i: (i, 0, 0, 0, 0)),
            pl.BlockSpec((per_step, degs, lats), lambda i: (i, 0, 0)),
        ],
        out_specs=pl.BlockSpec((dests, parts * waves, comps * levels * rows), lambda i: (0, 0, 0)),
        out_shape=jax.ShapeDtypeStruct((dests, parts * waves, comps * levels * rows), BF),
        scratch_shapes=[pltpu.VMEM((lats // LANES, lines * waves, LANES), F32)],
        compiler_params=params(),
        cost_estimate=pl.CostEstimate(
            flops=2 * lines * waves * degs * lats,
            bytes_accessed=2 * (legendre.size + 2 * spectral.size),
            transcendentals=0,
        ),
        name="legendre",
    )(first, spectral, legendre)


def tables_kernel(waves, wave_total, rates_ref, decay_ref, basis_ref, weight_ref):
    rows, lons = basis_ref.shape
    tracers, levels = decay_ref.shape
    both = tracers * levels
    lanes = LANES
    factor = 1.0 / math.sqrt(wave_total)
    chunk = divisor(rows, 96)

    def body(i, _):
        start = pl.multiple_of(i * chunk, chunk)
        row = start + lax.broadcasted_iota(jnp.int32, (chunk, lanes), 0)
        lon = lax.broadcasted_iota(jnp.int32, (chunk, lanes), 1)
        wave = row // (2 * waves) * waves + row % waves
        imag = row // waves % 2 == 1
        unit = 2.0 * math.pi / lons
        phase = (wave * lon % lons).astype(F32) * unit
        turn = (wave * lanes % lons).astype(F32) * unit
        c, s = jnp.cos(phase) * factor, jnp.sin(phase) * factor
        tc, ts = jnp.cos(turn), jnp.sin(turn)
        for j in range(lons // lanes):
            basis_ref[pl.ds(start, chunk), j * lanes : (j + 1) * lanes] = jnp.where(
                imag, -s, c
            ).astype(BF)
            c, s = c * tc - s * ts, s * tc + c * ts
        return 0

    lax.fori_loop(0, rows // chunk, body, 0)
    spread = (
        lax.broadcasted_iota(jnp.int32, (both, tracers), 0) // levels
        == lax.broadcasted_iota(jnp.int32, (both, tracers), 1)
    ).astype(F32)
    high = functools.partial(
        lax.dot_general, precision=lax.Precision.HIGHEST, preferred_element_type=F32
    )
    rows_of = high(spread, rates_ref[...], (((1,), (0,)), ((), ())))
    full = high(rows_of, spread, (((1,), (1,)), ((), ())))
    kept = high(spread, jnp.exp(-decay_ref[...]), (((1,), (0,)), ((), ())))
    own = lax.broadcasted_iota(jnp.int32, (both, levels), 0) % levels == lax.broadcasted_iota(
        jnp.int32, (both, levels), 1
    )
    kept = jnp.sum(jnp.where(own, kept, 0.0), axis=1, keepdims=True)
    row = lax.broadcasted_iota(jnp.int32, (both, both), 0)
    col = lax.broadcasted_iota(jnp.int32, (both, both), 1)
    full = jnp.where(row % levels == col % levels, full, 0.0)
    full = full + jnp.where(row == col, kept, 0.0)
    weight_ref[0] = full.astype(BF)
    weight_ref[1] = (full - full.astype(BF).astype(F32)).astype(BF)


def tables(rates, decay, waves, wave_total, lons):
    both = decay.shape[0] * decay.shape[1]
    return pl.pallas_call(
        functools.partial(tables_kernel, waves, wave_total),
        out_shape=(
            jax.ShapeDtypeStruct((2 * wave_total, lons), BF),
            jax.ShapeDtypeStruct((2, both, both), BF),
        ),
        compiler_params=params(),
        cost_estimate=pl.CostEstimate(
            flops=2 * wave_total * lons * 40, bytes_accessed=4 * wave_total * lons, transcendentals=0
        ),
        name="tables",
    )(rates, decay)


def winds_kernel(levels, rows, four_ref, basis_ref, winds_ref):
    cols = 256
    turned = four_ref[...].T
    comps = four_ref.shape[1] // (levels * rows)
    for j in range(basis_ref.shape[1] // cols):
        span = pl.ds(j * cols, cols)
        res = jnp.dot(turned, basis_ref[:, span], preferred_element_type=F32)
        res = res.astype(BF).astype(F32)
        for c in range(comps):
            for k in range(levels):
                first = (c * levels + k) * rows
                for h in range(cols // LANES):
                    tile = j * cols // LANES + h
                    winds_ref[tile, pl.ds(c * rows * levels + k, rows, stride=levels), :] = res[
                        first : first + rows, h * LANES : (h + 1) * LANES
                    ]


def wind_synthesis(received, basis, levels, rows):
    count = received.shape[1]
    return pl.pallas_call(
        functools.partial(winds_kernel, levels, rows),
        out_shape=jax.ShapeDtypeStruct((basis.shape[1] // LANES, count, LANES), F32),
        compiler_params=params(),
        cost_estimate=pl.CostEstimate(
            flops=2 * basis.size * count,
            bytes_accessed=2 * (basis.size + received.size) + 4 * count * basis.shape[1],
            transcendentals=0,
        ),
        name="winds",
    )(received, basis)


def limiter(speed):
    return COURANT * speed / (1.0 + jnp.abs(speed))


def twice(value):
    return jnp.concatenate([value, value], axis=0).astype(BF)


def advect_kernel(
    levels, weight_ref, q_ref, qn_ref, before_ref, after_ref, east_ref, north_ref, nb_ref, na_ref,
    out_ref, flux_ref, next_ref, gain_a, gain_b,
):
    step = pl.program_id(0)
    last = pl.num_programs(0) - 1
    rows, both, lons = q_ref.shape
    zero = jnp.zeros((), BF)
    pairs = [slice(s, s + 2 * levels) for s in range(0, both, 2 * levels)]

    @pl.when(step == 0)
    def _():
        face = twice(limiter(0.5 * (tiles(nb_ref, 0, levels) + tiles(north_ref, 0, levels))))
        for p in pairs:
            flux_ref[p] = face * jnp.where(face > zero, before_ref[0, p], q_ref[0, p])

    @pl.when(step == last)
    def _():
        next_ref[...] = after_ref[0]

    @pl.when(step != last)
    def _():
        next_ref[...] = qn_ref[0]

    lat = step * rows
    total = north_ref.shape[1] // levels
    gains = [gain_a, gain_b]
    for r in range(rows + 1):
        if r < rows:
            east = tiles(east_ref, r * levels, levels)
            face = limiter(0.5 * (east + pltpu.roll(east, lons - 1, 1)))
            cx, cw = twice(face), twice(pltpu.roll(face, 1, 1))
            here = tiles(north_ref, pl.multiple_of((lat + r) * levels, levels), levels)
            if r < rows - 1:
                there = tiles(north_ref, pl.multiple_of((lat + r + 1) * levels, levels), levels)
            else:
                inside = jnp.minimum(lat + r + 1, total - 1)
                there = tiles(north_ref, pl.multiple_of(inside * levels, levels), levels)
                there = jnp.where(step == last, tiles(na_ref, 0, levels), there)
            cy = twice(limiter(0.5 * (here + there)))
            mx, mw, my = cx > zero, cw > zero, cy > zero
            for p in pairs:
                q0 = q_ref[r, p]
                q1 = q_ref[r + 1, p] if r < rows - 1 else next_ref[p]
                fx = cx * jnp.where(mx, q0, pltpu.roll(q0, lons - 1, 1))
                fw = cw * jnp.where(mw, pltpu.roll(q0, 1, 1), q0)
                fy = cy * jnp.where(my, q0, q1)
                gains[r % 2][p] = (fw - fx) + (flux_ref[p] - fy)
                flux_ref[p] = fy
        if r > 0:
            q0, gain = q_ref[r - 1], gains[(r - 1) % 2][...]
            out_ref[r - 1] = (
                jnp.dot(weight_ref[0], q0, preferred_element_type=F32)
                + jnp.dot(weight_ref[1], q0, preferred_element_type=F32)
                + jnp.dot(weight_ref[0], gain, preferred_element_type=F32)
            ).astype(BF)


def advect(weight, q, before, after, winds, north_before, north_after, levels):
    total, both, lons = q.shape
    rows = divisor(total, 6)
    whole = lambda *shape: pl.BlockSpec(shape, lambda i: (0,) * len(shape))
    return pl.pallas_call(
        functools.partial(advect_kernel, levels),
        grid=(total // rows,),
        in_specs=[
            whole(2, both, both),
            pl.BlockSpec((rows, both, lons), lambda i: (i, 0, 0)),
            pl.BlockSpec((1, both, lons), lambda i: (jnp.minimum(rows * (i + 1), total - 1), 0, 0)),
            whole(1, both, lons),
            whole(1, both, lons),
            pl.BlockSpec((lons // LANES, rows * levels, LANES), lambda i: (0, i, 0)),
            pl.BlockSpec((lons // LANES, total * levels, LANES), lambda i: (0, 1, 0)),
            whole(lons // LANES, levels, LANES),
            whole(lons // LANES, levels, LANES),
        ],
        out_specs=pl.BlockSpec((rows, both, lons), lambda i: (i, 0, 0)),
        out_shape=jax.ShapeDtypeStruct(q.shape, BF),
        scratch_shapes=[pltpu.VMEM((both, lons), BF)] * 4,
        compiler_params=params(),
        cost_estimate=pl.CostEstimate(
            flops=2 * both * q.size, bytes_accessed=5 * q.size, transcendentals=0
        ),
        name="advect",
    )(weight, q, q, before, after, winds, winds, north_before, north_after)


def shards(spectral, legendre, tracers, rates, decay):
    waves, _, comps, levels, _ = spectral.shape
    rows, tracer_count, _, lons = tracers.shape
    devices = lax.axis_size("lat")
    me = lax.axis_index("lat")
    up = [(i, i + 1) for i in range(devices - 1)]
    down = [(j, i) for i, j in up]
    q = tracers.reshape(rows, tracer_count * levels, lons)
    before = lax.ppermute(q[-1:], "lat", up)
    after = lax.ppermute(q[:1], "lat", down)
    first = jnp.full((1,), me * waves, jnp.int32)
    fourier = legendre_synthesis(first, spectral, legendre, devices)
    before, after, fourier = lax.optimization_barrier((before, after, fourier))
    received = lax.all_to_all(fourier, "lat", split_axis=0, concat_axis=0, tiled=True)
    basis, weight = tables(rates, decay, waves, waves * devices, lons)
    received = received.reshape(devices * 2 * waves, comps * levels * rows)
    winds = wind_synthesis(received, basis, levels, rows)
    north_before = lax.ppermute(winds[:, -levels:], "lat", up)
    north_after = lax.ppermute(winds[:, rows * levels : (rows + 1) * levels], "lat", down)
    out = advect(weight, q, before, after, winds, north_before, north_after, levels)
    return out.reshape(tracers.shape)


def solution(mesh):
    in_specs = (
        P("lat", None, None, "groups", None),
        P("lat", None, None),
        P("lat", None, "groups", None),
        P(),
        P(),
    )
    out_specs = P("lat", None, "groups", None)
    return jax.shard_map(shards, mesh=mesh, in_specs=in_specs, out_specs=out_specs, check_vma=False)
```

```python
import functools
import math

import jax
import jax.numpy as jnp
from jax import lax
from jax.experimental import pallas as pl
from jax.experimental.pallas import tpu as pltpu
from jax.sharding import PartitionSpec as P

COURANT = 0.45
BF = jnp.bfloat16
F32 = jnp.float32
LANES = 128


def divisor(count, most):
    return max(d for d in range(1, most + 1) if count % d == 0)


def tiles(ref, first, count):
    return jnp.concatenate([ref[j, pl.ds(first, count), :] for j in range(ref.shape[0])], axis=1)


def wave_group(waves):
    return divisor(waves, 8)


def params(mebibytes):
    return pltpu.CompilerParams(vmem_limit_bytes=mebibytes * 2**20)


def legendre_kernel(windows, rows, first_ref, spec_ref, leg_ref, *refs):
    *out_refs, four_ref = refs
    step = pl.program_id(0)
    group, _, _, levels, degs = spec_ref.shape
    lats = leg_ref.shape[2]
    lines = spec_ref.shape[1] * spec_ref.shape[2] * levels
    deg = lax.broadcasted_iota(jnp.int32, (lines, degs), 1)
    for i in range(group):
        coeffs = spec_ref[i].astype(F32).reshape(lines, degs)
        coeffs = jnp.where(deg >= first_ref[0] + step * group + i, coeffs, 0.0).astype(BF)
        res = jnp.dot(coeffs, leg_ref[i], preferred_element_type=F32)
        for j in range(lats // LANES):
            four_ref[j, pl.ds(i, lines, stride=group), :] = res[:, j * LANES : (j + 1) * LANES]
    half = lines // 2
    for ck in range(half):
        both = jnp.concatenate(
            [tiles(four_ref, first, group) for first in (ck * group, (half + ck) * group)], axis=0
        ).astype(BF)
        for (begin, width), out_ref in zip(windows, out_refs):
            for d in range(lats // rows):
                low, high = d * rows + begin, d * rows + begin + width
                inside = both[:, max(low, 0) : min(high, lats)]
                if low < 0 or high > lats:
                    out_ref[d, :, ck * width : (ck + 1) * width] = jnp.zeros((2 * group, width), BF)
                lane = ck * width + max(-low, 0)
                out_ref[d, :, lane : lane + inside.shape[1]] = inside


def legendre_synthesis(first, spectral, legendre, windows, rows):
    waves, parts, comps, levels, degs = spectral.shape
    lats = legendre.shape[2]
    dests = lats // rows
    group = wave_group(waves)
    lines = parts * comps * levels
    widths = [comps * levels * width for _, width in windows]
    return pl.pallas_call(
        functools.partial(legendre_kernel, windows, rows),
        grid=(waves // group,),
        in_specs=[
            pl.BlockSpec(memory_space=pltpu.SMEM),
            pl.BlockSpec((group, parts, comps, levels, degs), lambda i: (i, 0, 0, 0, 0)),
            pl.BlockSpec((group, degs, lats), lambda i: (i, 0, 0)),
        ],
        out_specs=[pl.BlockSpec((dests, parts * group, w), lambda i: (0, i, 0)) for w in widths],
        out_shape=[jax.ShapeDtypeStruct((dests, parts * waves, w), BF) for w in widths],
        scratch_shapes=[pltpu.VMEM((lats // LANES, lines * group, LANES), F32)],
        compiler_params=params(56),
        cost_estimate=pl.CostEstimate(
            flops=2 * lines * waves * degs * lats,
            bytes_accessed=2 * (legendre.size + 2 * spectral.size),
            transcendentals=0,
        ),
        name="legendre",
    )(first, spectral, legendre)


def tables_kernel(waves, wave_total, rates_ref, decay_ref, basis_ref, weight_ref):
    rows, lons = basis_ref.shape
    tracers, levels = decay_ref.shape
    both = tracers * levels
    lanes = LANES
    factor = 1.0 / math.sqrt(wave_total)
    chunk = divisor(rows, 96)

    def body(i, _):
        start = pl.multiple_of(i * chunk, chunk)
        row = start + lax.broadcasted_iota(jnp.int32, (chunk, lanes), 0)
        lon = lax.broadcasted_iota(jnp.int32, (chunk, lanes), 1)
        group = wave_group(waves)
        wave = row // (2 * group) * group + row % group
        imag = row // group % 2 == 1
        unit = 2.0 * math.pi / lons
        phase = (wave * lon % lons).astype(F32) * unit
        turn = (wave * lanes % lons).astype(F32) * unit
        c, s = jnp.cos(phase) * factor, jnp.sin(phase) * factor
        tc, ts = jnp.cos(turn), jnp.sin(turn)
        for j in range(lons // lanes):
            basis_ref[pl.ds(start, chunk), j * lanes : (j + 1) * lanes] = jnp.where(
                imag, -s, c
            ).astype(BF)
            c, s = c * tc - s * ts, s * tc + c * ts
        return 0

    lax.fori_loop(0, rows // chunk, body, 0)
    spread = (
        lax.broadcasted_iota(jnp.int32, (both, tracers), 0) // levels
        == lax.broadcasted_iota(jnp.int32, (both, tracers), 1)
    ).astype(F32)
    high = functools.partial(
        lax.dot_general, precision=lax.Precision.HIGHEST, preferred_element_type=F32
    )
    rows_of = high(spread, rates_ref[...], (((1,), (0,)), ((), ())))
    full = high(rows_of, spread, (((1,), (1,)), ((), ())))
    kept = high(spread, jnp.exp(-decay_ref[...]), (((1,), (0,)), ((), ())))
    own = lax.broadcasted_iota(jnp.int32, (both, levels), 0) % levels == lax.broadcasted_iota(
        jnp.int32, (both, levels), 1
    )
    kept = jnp.sum(jnp.where(own, kept, 0.0), axis=1, keepdims=True)
    row = lax.broadcasted_iota(jnp.int32, (both, both), 0)
    col = lax.broadcasted_iota(jnp.int32, (both, both), 1)
    full = jnp.where(row % levels == col % levels, full, 0.0)
    full = full + jnp.where(row == col, kept, 0.0)
    weight_ref[0] = full.astype(BF)
    weight_ref[1] = (full - full.astype(BF).astype(F32)).astype(BF)


def tables(rates, decay, waves, wave_total, lons):
    both = decay.shape[0] * decay.shape[1]
    return pl.pallas_call(
        functools.partial(tables_kernel, waves, wave_total),
        out_shape=(
            jax.ShapeDtypeStruct((2 * wave_total, lons), BF),
            jax.ShapeDtypeStruct((2, both, both), BF),
        ),
        compiler_params=params(56),
        cost_estimate=pl.CostEstimate(
            flops=2 * wave_total * lons * 40, bytes_accessed=4 * wave_total * lons, transcendentals=0
        ),
        name="tables",
    )(rates, decay)


def limiter(speed):
    return COURANT * speed / (1.0 + jnp.abs(speed))


def twice(value):
    return jnp.concatenate([value, value], axis=0).astype(BF)


def synthesize(levels, four_ref, basis_ref, turned_ref, east_ref, north_ref):
    turned_ref[...] = four_ref[...].T
    rows = east_ref.shape[1] // levels
    cols = 2
    for j in range(east_ref.shape[0] // cols):
        span = slice(j * cols * LANES, (j + 1) * cols * LANES)
        res = jnp.dot(turned_ref[...], basis_ref[:, span], preferred_element_type=F32)
        res = res.astype(BF).astype(F32)
        for h in range(cols):
            tile = res[:, h * LANES : (h + 1) * LANES]
            for c, ref in enumerate((east_ref, north_ref)):
                for k in range(levels):
                    first = (c * levels + k) * rows
                    ref[j * cols + h, pl.ds(k, rows, stride=levels), :] = tile[first : first + rows]


def advect_kernel(levels, first, begin, ends, weight_ref, q_ref, qn_ref, prev_ref, *refs):
    after_refs, refs = (refs[:1], refs[1:]) if ends else ((), refs)
    four_ref, basis_ref, *refs = refs
    out_ref, flux_ref, next_ref, gain_a, gain_b, turned_ref, east_ref, north_ref = refs[-8:]
    step = pl.program_id(0)
    rows, both, lons = q_ref.shape
    zero = jnp.zeros((), BF)
    pairs = [slice(s, s + 2 * levels) for s in range(0, both, 2 * levels)]

    def wind(ref, row):
        start = (step * rows + first + row - begin) * levels
        return tiles(ref, pl.multiple_of(start, levels), levels)

    @pl.when(step == 0)
    def _():
        synthesize(levels, four_ref, basis_ref, turned_ref, east_ref, north_ref)
        face = twice(limiter(0.5 * (wind(north_ref, -1) + wind(north_ref, 0))))
        for p in pairs:
            flux_ref[p] = face * jnp.where(face > zero, prev_ref[0, p], q_ref[0, p])

    if ends:
        last = pl.num_programs(0) - 1

        @pl.when(step == last)
        def _():
            next_ref[...] = after_refs[0][0]

        @pl.when(step != last)
        def _():
            next_ref[...] = qn_ref[0]

    gains = [gain_a, gain_b]
    for r in range(rows + 1):
        if r < rows:
            east = wind(east_ref, r)
            face = limiter(0.5 * (east + pltpu.roll(east, lons - 1, 1)))
            cx, cw = twice(face), twice(pltpu.roll(face, 1, 1))
            cy = twice(limiter(0.5 * (wind(north_ref, r) + wind(north_ref, r + 1))))
            mx, mw, my = cx > zero, cw > zero, cy > zero
            for p in pairs:
                q0 = q_ref[r, p]
                if r < rows - 1:
                    q1 = q_ref[r + 1, p]
                else:
                    q1 = next_ref[p] if ends else qn_ref[0, p]
                fx = cx * jnp.where(mx, q0, pltpu.roll(q0, lons - 1, 1))
                fw = cw * jnp.where(mw, pltpu.roll(q0, 1, 1), q0)
                fy = cy * jnp.where(my, q0, q1)
                gains[r % 2][p] = (fw - fx) + (flux_ref[p] - fy)
                flux_ref[p] = fy
        if r > 0:
            q0, gain = q_ref[r - 1], gains[(r - 1) % 2][...]
            out_ref[r - 1] = (
                jnp.dot(weight_ref[0], q0, preferred_element_type=F32)
                + jnp.dot(weight_ref[1], q0, preferred_element_type=F32)
                + jnp.dot(weight_ref[0], gain, preferred_element_type=F32)
            ).astype(BF)


def advect(weight, q, prev, after, fourier, basis, levels, rows, first, count, begin, done):
    total, both, lons = q.shape
    base = first // rows
    ends = first + rows * count == total
    whole = lambda *shape: pl.BlockSpec(
        shape, lambda i: (0,) * len(shape), pipeline_mode=pl.Buffered(1)
    )
    winds = pltpu.VMEM((lons // LANES, fourier.shape[1] // 2, LANES), F32)
    one = lambda index: pl.BlockSpec((1, both, lons), lambda i: (index(i), 0, 0))
    operands = [weight, q, q, prev if first == 0 else q, *[after] * ends, fourier, basis]
    in_specs = [
        whole(2, both, both),
        pl.BlockSpec((rows, both, lons), lambda i: (i + base, 0, 0)),
        one(lambda i: jnp.minimum(rows * (i + base + 1), total - 1)),
        pl.BlockSpec(
            (1, both, lons), lambda i: (max(first - 1, 0), 0, 0), pipeline_mode=pl.Buffered(1)
        ),
        *[whole(1, both, lons)] * ends,
        whole(*fourier.shape),
        whole(*basis.shape),
    ]
    aliases = {}
    if done is not None:
        aliases = {len(operands): 0}
        operands.append(done)
        in_specs.append(pl.BlockSpec(memory_space=pl.ANY))
    return pl.pallas_call(
        functools.partial(advect_kernel, levels, first, begin, ends),
        grid=(count,),
        in_specs=in_specs,
        out_specs=pl.BlockSpec((rows, both, lons), lambda i: (i + base, 0, 0)),
        out_shape=jax.ShapeDtypeStruct(q.shape, BF),
        scratch_shapes=[pltpu.VMEM((both, lons), BF)] * 4
        + [pltpu.VMEM(fourier.shape[::-1], BF), winds, winds],
        input_output_aliases=aliases,
        compiler_params=params(56),
        cost_estimate=pl.CostEstimate(
            flops=6 * both * rows * count * both * lons,
            bytes_accessed=5 * rows * count * both * lons,
            transcendentals=0,
        ),
        name="advect",
    )(*operands)


def exchange(value):
    devices, lines, width = value.shape
    received = lax.all_to_all(value, "lat", split_axis=0, concat_axis=0, tiled=True)
    return received.reshape(devices * lines, width)


def shards(spectral, legendre, tracers, rates, decay):
    waves, _, comps, levels, _ = spectral.shape
    rows, tracer_count, _, lons = tracers.shape
    devices = lax.axis_size("lat")
    up = [(i, i + 1) for i in range(devices - 1)]
    down = [(j, i) for i, j in up]
    per_step = divisor(rows, 6)
    blocks = rows // per_step
    counts = [blocks] if blocks < 4 else [blocks * 3 // 8, blocks - blocks * 3 // 8]
    firsts = [per_step * sum(counts[:i]) for i in range(len(counts))]
    windows = []
    for start, count in zip(firsts, counts):
        width = pl.cdiv(per_step * count + 2, 8) * 8
        windows.append((min(start - 1, rows + 1 - width) if start > 0 else -1, width))
    q = tracers.reshape(rows, tracer_count * levels, lons)
    before, after = lax.ppermute(q[-1:], "lat", up), lax.ppermute(q[:1], "lat", down)
    first = jnp.full((1,), lax.axis_index("lat") * waves, jnp.int32)
    sent = list(legendre_synthesis(first, spectral, legendre, windows, rows))
    basis, weight = tables(rates, decay, waves, waves * devices, lons)
    received = []
    for i in range(len(sent)):
        if i > 0:
            received[-1], sent[i], weight = lax.optimization_barrier((received[-1], sent[i], weight))
        received.append(exchange(sent[i]))
    done = None
    for fourier, start, count, (begin, _) in zip(received, firsts, counts, windows):
        done = advect(
            weight, q, before, after, fourier, basis, levels, per_step, start, count, begin, done
        )
    return done.reshape(tracers.shape)


def solution(mesh):
    in_specs = (
        P("lat", None, None, "groups", None),
        P("lat", None, None),
        P("lat", None, "groups", None),
        P(),
        P(),
    )
    out_specs = P("lat", None, "groups", None)
    return jax.shard_map(shards, mesh=mesh, in_specs=in_specs, out_specs=out_specs, check_vma=False)
```

```python
import functools
import math

import jax
import jax.numpy as jnp
from jax import lax
from jax.experimental import pallas as pl
from jax.experimental.pallas import tpu as pltpu
from jax.sharding import PartitionSpec as P

COURANT = 0.45
BF = jnp.bfloat16
F32 = jnp.float32
LANES = 128


def divisor(count, most):
    return max(d for d in range(1, most + 1) if count % d == 0)


def tiles(ref, first, count):
    return jnp.concatenate([ref[j, pl.ds(first, count), :] for j in range(ref.shape[0])], axis=1)


def wave_group(waves):
    return divisor(waves, 8)


def params(mebibytes):
    return pltpu.CompilerParams(vmem_limit_bytes=mebibytes * 2**20)


def legendre_kernel(windows, rows, first_ref, spec_ref, leg_ref, *refs):
    *out_refs, four_ref = refs
    step = pl.program_id(0)
    group, _, _, levels, degs = spec_ref.shape
    lats = leg_ref.shape[2]
    lines = spec_ref.shape[1] * spec_ref.shape[2] * levels
    deg = lax.broadcasted_iota(jnp.int32, (lines, degs), 1)
    for i in range(group):
        coeffs = spec_ref[i].astype(F32).reshape(lines, degs)
        coeffs = jnp.where(deg >= first_ref[0] + step * group + i, coeffs, 0.0).astype(BF)
        res = jnp.dot(coeffs, leg_ref[i], preferred_element_type=F32)
        for j in range(lats // LANES):
            four_ref[j, pl.ds(i, lines, stride=group), :] = res[:, j * LANES : (j + 1) * LANES]
    half = lines // 2
    for ck in range(half):
        both = jnp.concatenate(
            [tiles(four_ref, first, group) for first in (ck * group, (half + ck) * group)], axis=0
        ).astype(BF)
        for (begin, width), out_ref in zip(windows, out_refs):
            for d in range(lats // rows):
                low, high = d * rows + begin, d * rows + begin + width
                inside = both[:, max(low, 0) : min(high, lats)]
                if low < 0 or high > lats:
                    out_ref[d, :, ck * width : (ck + 1) * width] = jnp.zeros((2 * group, width), BF)
                lane = ck * width + max(-low, 0)
                out_ref[d, :, lane : lane + inside.shape[1]] = inside


def legendre_synthesis(first, spectral, legendre, windows, rows):
    waves, parts, comps, levels, degs = spectral.shape
    lats = legendre.shape[2]
    dests = lats // rows
    group = wave_group(waves)
    lines = parts * comps * levels
    widths = [comps * levels * width for _, width in windows]
    return pl.pallas_call(
        functools.partial(legendre_kernel, windows, rows),
        grid=(waves // group,),
        in_specs=[
            pl.BlockSpec(memory_space=pltpu.SMEM),
            pl.BlockSpec((group, parts, comps, levels, degs), lambda i: (i, 0, 0, 0, 0)),
            pl.BlockSpec((group, degs, lats), lambda i: (i, 0, 0)),
        ],
        out_specs=[pl.BlockSpec((dests, parts * group, w), lambda i: (0, i, 0)) for w in widths],
        out_shape=[jax.ShapeDtypeStruct((dests, parts * waves, w), BF) for w in widths],
        scratch_shapes=[pltpu.VMEM((lats // LANES, lines * group, LANES), F32)],
        compiler_params=params(56),
        cost_estimate=pl.CostEstimate(
            flops=2 * lines * waves * degs * lats,
            bytes_accessed=2 * (legendre.size + 2 * spectral.size),
            transcendentals=0,
        ),
        name="legendre",
    )(first, spectral, legendre)


def tables_kernel(waves, wave_total, rates_ref, decay_ref, basis_ref, weight_ref):
    rows, lons = basis_ref.shape
    tracers, levels = decay_ref.shape
    both = tracers * levels
    lanes = LANES
    factor = 1.0 / math.sqrt(wave_total)
    chunk = divisor(rows, 96)

    def body(i, _):
        start = pl.multiple_of(i * chunk, chunk)
        row = start + lax.broadcasted_iota(jnp.int32, (chunk, lanes), 0)
        lon = lax.broadcasted_iota(jnp.int32, (chunk, lanes), 1)
        group = wave_group(waves)
        wave = row // (2 * group) * group + row % group
        imag = row // group % 2 == 1
        unit = 2.0 * math.pi / lons
        phase = (wave * lon % lons).astype(F32) * unit
        turn = (wave * lanes % lons).astype(F32) * unit
        c, s = jnp.cos(phase) * factor, jnp.sin(phase) * factor
        tc, ts = jnp.cos(turn), jnp.sin(turn)
        for j in range(lons // lanes):
            basis_ref[pl.ds(start, chunk), j * lanes : (j + 1) * lanes] = jnp.where(
                imag, -s, c
            ).astype(BF)
            c, s = c * tc - s * ts, s * tc + c * ts
        return 0

    lax.fori_loop(0, rows // chunk, body, 0)
    spread = (
        lax.broadcasted_iota(jnp.int32, (both, tracers), 0) // levels
        == lax.broadcasted_iota(jnp.int32, (both, tracers), 1)
    ).astype(F32)
    high = functools.partial(
        lax.dot_general, precision=lax.Precision.HIGHEST, preferred_element_type=F32
    )
    rows_of = high(spread, rates_ref[...], (((1,), (0,)), ((), ())))
    full = high(rows_of, spread, (((1,), (1,)), ((), ())))
    kept = high(spread, jnp.exp(-decay_ref[...]), (((1,), (0,)), ((), ())))
    own = lax.broadcasted_iota(jnp.int32, (both, levels), 0) % levels == lax.broadcasted_iota(
        jnp.int32, (both, levels), 1
    )
    kept = jnp.sum(jnp.where(own, kept, 0.0), axis=1, keepdims=True)
    row = lax.broadcasted_iota(jnp.int32, (both, both), 0)
    col = lax.broadcasted_iota(jnp.int32, (both, both), 1)
    full = jnp.where(row % levels == col % levels, full, 0.0)
    full = full + jnp.where(row == col, kept, 0.0)
    weight_ref[0] = full.astype(BF)
    weight_ref[1] = (full - full.astype(BF).astype(F32)).astype(BF)


def tables(rates, decay, waves, wave_total, lons):
    both = decay.shape[0] * decay.shape[1]
    return pl.pallas_call(
        functools.partial(tables_kernel, waves, wave_total),
        out_shape=(
            jax.ShapeDtypeStruct((2 * wave_total, lons), BF),
            jax.ShapeDtypeStruct((2, both, both), BF),
        ),
        compiler_params=params(56),
        cost_estimate=pl.CostEstimate(
            flops=2 * wave_total * lons * 40, bytes_accessed=4 * wave_total * lons, transcendentals=0
        ),
        name="tables",
    )(rates, decay)


def limiter(speed):
    return COURANT * speed / (1.0 + jnp.abs(speed))


def twice(value):
    return jnp.concatenate([value, value], axis=0).astype(BF)


def synthesize(levels, four_ref, basis_ref, turned_ref, east_ref, north_ref):
    turned_ref[...] = four_ref[...].T
    rows = east_ref.shape[1] // levels
    cols = 2
    for j in range(east_ref.shape[0] // cols):
        span = slice(j * cols * LANES, (j + 1) * cols * LANES)
        res = jnp.dot(turned_ref[...], basis_ref[:, span], preferred_element_type=F32)
        res = res.astype(BF).astype(F32)
        for h in range(cols):
            tile = res[:, h * LANES : (h + 1) * LANES]
            for c, ref in enumerate((east_ref, north_ref)):
                for k in range(levels):
                    first = (c * levels + k) * rows
                    ref[j * cols + h, pl.ds(k, rows, stride=levels), :] = tile[first : first + rows]


def advect_kernel(levels, first, begin, ends, weight_ref, q_ref, qn_ref, prev_ref, *refs):
    after_refs, refs = (refs[:1], refs[1:]) if ends else ((), refs)
    four_ref, basis_ref, *refs = refs
    out_ref, flux_ref, next_ref, gain_a, gain_b, turned_ref, east_ref, north_ref = refs[-8:]
    step = pl.program_id(0)
    rows, both, lons = q_ref.shape
    zero = jnp.zeros((), BF)
    pairs = [slice(s, s + 2 * levels) for s in range(0, both, 2 * levels)]

    def wind(ref, row):
        start = (step * rows + first + row - begin) * levels
        return tiles(ref, pl.multiple_of(start, levels), levels)

    @pl.when(step == 0)
    def _():
        synthesize(levels, four_ref, basis_ref, turned_ref, east_ref, north_ref)
        face = twice(limiter(0.5 * (wind(north_ref, -1) + wind(north_ref, 0))))
        for p in pairs:
            flux_ref[p] = face * jnp.where(face > zero, prev_ref[0, p], q_ref[0, p])

    if ends:
        last = pl.num_programs(0) - 1

        @pl.when(step == last)
        def _():
            next_ref[...] = after_refs[0][0]

        @pl.when(step != last)
        def _():
            next_ref[...] = qn_ref[0]

    gains = [gain_a, gain_b]
    for r in range(rows + 1):
        if r < rows:
            east = wind(east_ref, r)
            face = limiter(0.5 * (east + pltpu.roll(east, lons - 1, 1)))
            cx, cw = twice(face), twice(pltpu.roll(face, 1, 1))
            cy = twice(limiter(0.5 * (wind(north_ref, r) + wind(north_ref, r + 1))))
            mx, mw, my = cx > zero, cw > zero, cy > zero
            for p in pairs:
                q0 = q_ref[r, p]
                if r < rows - 1:
                    q1 = q_ref[r + 1, p]
                else:
                    q1 = next_ref[p] if ends else qn_ref[0, p]
                fx = cx * jnp.where(mx, q0, pltpu.roll(q0, lons - 1, 1))
                fw = cw * jnp.where(mw, pltpu.roll(q0, 1, 1), q0)
                fy = cy * jnp.where(my, q0, q1)
                gains[r % 2][p] = (fw - fx) + (flux_ref[p] - fy)
                flux_ref[p] = fy
        if r > 0:
            q0, gain = q_ref[r - 1], gains[(r - 1) % 2][...]
            out_ref[r - 1] = (
                jnp.dot(weight_ref[0], q0, preferred_element_type=F32)
                + jnp.dot(weight_ref[1], q0, preferred_element_type=F32)
                + jnp.dot(weight_ref[0], gain, preferred_element_type=F32)
            ).astype(BF)


def advect(weight, q, prev, after, fourier, basis, levels, rows, first, count, begin, done):
    total, both, lons = q.shape
    base = first // rows
    ends = first + rows * count == total
    whole = lambda *shape: pl.BlockSpec(
        shape, lambda i: (0,) * len(shape), pipeline_mode=pl.Buffered(1)
    )
    winds = pltpu.VMEM((lons // LANES, fourier.shape[1] // 2, LANES), F32)
    one = lambda index: pl.BlockSpec((1, both, lons), lambda i: (index(i), 0, 0))
    operands = [weight, q, q, prev if first == 0 else q, *[after] * ends, fourier, basis]
    in_specs = [
        whole(2, both, both),
        pl.BlockSpec((rows, both, lons), lambda i: (i + base, 0, 0)),
        one(lambda i: jnp.minimum(rows * (i + base + 1), total - 1)),
        pl.BlockSpec(
            (1, both, lons), lambda i: (max(first - 1, 0), 0, 0), pipeline_mode=pl.Buffered(1)
        ),
        *[whole(1, both, lons)] * ends,
        whole(*fourier.shape),
        whole(*basis.shape),
    ]
    aliases = {}
    if done is not None:
        aliases = {len(operands): 0}
        operands.append(done)
        in_specs.append(pl.BlockSpec(memory_space=pl.ANY))
    return pl.pallas_call(
        functools.partial(advect_kernel, levels, first, begin, ends),
        grid=(count,),
        in_specs=in_specs,
        out_specs=pl.BlockSpec((rows, both, lons), lambda i: (i + base, 0, 0)),
        out_shape=jax.ShapeDtypeStruct(q.shape, BF),
        scratch_shapes=[pltpu.VMEM((both, lons), BF)] * 4
        + [pltpu.VMEM(fourier.shape[::-1], BF), winds, winds],
        input_output_aliases=aliases,
        compiler_params=params(56),
        cost_estimate=pl.CostEstimate(
            flops=6 * both * rows * count * both * lons,
            bytes_accessed=5 * rows * count * both * lons,
            transcendentals=0,
        ),
        name="advect",
    )(*operands)


def exchange(value):
    devices, lines, width = value.shape
    received = lax.all_to_all(value, "lat", split_axis=0, concat_axis=0, tiled=True)
    return received.reshape(devices * lines, width)


def shards(spectral, legendre, tracers, rates, decay):
    waves, _, comps, levels, _ = spectral.shape
    rows, tracer_count, _, lons = tracers.shape
    devices = lax.axis_size("lat")
    up = [(i, i + 1) for i in range(devices - 1)]
    down = [(j, i) for i, j in up]
    per_step = divisor(rows, 4)
    blocks = rows // per_step
    counts = [blocks] if blocks < 4 else [blocks * 5 // 12, blocks - blocks * 5 // 12]
    firsts = [per_step * sum(counts[:i]) for i in range(len(counts))]
    windows = []
    for start, count in zip(firsts, counts):
        width = pl.cdiv(per_step * count + 2, 8) * 8
        windows.append((min(start - 1, rows + 1 - width) if start > 0 else -1, width))
    q = tracers.reshape(rows, tracer_count * levels, lons)
    before, after = lax.ppermute(q[-1:], "lat", up), lax.ppermute(q[:1], "lat", down)
    first = jnp.full((1,), lax.axis_index("lat") * waves, jnp.int32)
    sent = list(legendre_synthesis(first, spectral, legendre, windows, rows))
    basis, weight = tables(rates, decay, waves, waves * devices, lons)
    received = []
    for i in range(len(sent)):
        if i > 0:
            received[-1], sent[i], weight = lax.optimization_barrier((received[-1], sent[i], weight))
        received.append(exchange(sent[i]))
    done = None
    for fourier, start, count, (begin, _) in zip(received, firsts, counts, windows):
        done = advect(
            weight, q, before, after, fourier, basis, levels, per_step, start, count, begin, done
        )
    return done.reshape(tracers.shape)


def solution(mesh):
    in_specs = (
        P("lat", None, None, "groups", None),
        P("lat", None, None),
        P("lat", None, "groups", None),
        P(),
        P(),
    )
    out_specs = P("lat", None, "groups", None)
    return jax.shard_map(shards, mesh=mesh, in_specs=in_specs, out_specs=out_specs, check_vma=False)
```
